32 devices in a mesh: slide: 2 (over y), seq: 8 (over z, x), head: 2 (over core).
Axes of the slice: x: 2, y: 2, z: 4, core: 2. Of those that a mesh axis runs over, the one named last changes fastest.
Arguments:
- tokens: bfloat16 [8192, 768], P(('slide', 'seq')), parts along dimension 0
- tile_index: int32 [8192], P(('slide', 'seq')), parts along dimension 0, may hold values from 0 to 8191, as said below
- dilation_offset: int32 [2, 16], P(None, 'head'), may hold values from 0 to 3, as said below
- norm_gain: float32 [768], replicated
- w_query: bfloat16 [768, 768], P(None, 'head'), may hold values from -0.21875 to 0.21875
- w_key: bfloat16 [768, 768], P(None, 'head'), may hold values from -0.21875 to 0.21875
- w_value: bfloat16 [768, 768], P(None, 'head'), may hold values from -0.21875 to 0.21875
- w_out: bfloat16 [768, 768], P('head'), may hold values from -0.21875 to 0.21875
Outputs:
- mixed: float32 [8192, 768], P(('slide', 'seq'), 'head'), parts along dimension 0
The draws below stay inside these ranges and needn't reach their ends.
There are 2 independent parts, one for each index of `slide`. The reference program is written for one: setup_inputs(seed, part) draws one part's arguments, and reference() takes and returns one part's arrays. A program takes and returns all parts, laid end to end along the dimension named above; an argument that names none is the same for every part. Nothing has to cross between parts.
Inputs may be any that keep to these rules, and one draw needn't show every extreme that they name: `tile_index`: strictly rising along a slide; tile p holds 2 p or 2 p + 1, the first holds 0 and the last 8191. `dilation_offset`: row 0 is below 2 and holds 1 at some head; row 1 is below 4 and holds 3 at some head (2 and 4 follow the number of devices along seq as the steps state).
All inputs are finite; a program needn't handle non-finite values.
Results may differ from the reference program's by a relative error of at most 0.0074.
Values may be sent and summed in bfloat16 or wider, within the bound.
A program may use at most 64 MiB of HBM per device.

```python
import jax
import jax.numpy as jnp
from jax import lax

D = 768
HEADS = 16
HEAD_DIM = 48
BLOCK = 1024
R2 = 2
R3 = 4
SEQ = 4096
GRID_W = 256


def draw_tokens(key, part):
    key = jax.random.fold_in(key, 11)
    key_base = jax.random.fold_in(key, 0)
    base = jnp.clip(jax.random.normal(key_base, (SEQ, D), jnp.float32), -6.0, 6.0)
    return base.astype(jnp.bfloat16)


def draw_norm_gain(key, part):
    key = jax.random.fold_in(key, 23)
    key_base = jax.random.fold_in(key, 0)
    base = 1.0 + 0.1 * jnp.clip(jax.random.normal(key_base, (D,), jnp.float32), -4.0, 4.0)
    return base.astype(jnp.float32)


def draw_tile_index(key, part):
    key = jax.random.fold_in(key, 37)
    bits = jax.random.randint(key, (SEQ,), 0, 2)
    bits = bits.at[0].set(0).at[SEQ - 1].set(1)
    return (2 * jnp.arange(SEQ, dtype=jnp.int32) + bits).astype(jnp.int32)


def draw_dilation_offset(key, part):
    key = jax.random.fold_in(key, 53)
    key_a, key_b, key_c, key_d = jax.random.split(key, 4)
    row_two = jax.random.randint(key_a, (HEADS,), 0, R2)
    row_three = jax.random.randint(key_b, (HEADS,), 0, R3)
    heads = jnp.arange(HEADS)
    row_two = jnp.where(heads == jax.random.randint(key_c, (), 0, HEADS), R2 - 1, row_two)
    row_three = jnp.where(heads == jax.random.randint(key_d, (), 0, HEADS), R3 - 1, row_three)
    return jnp.stack([row_two, row_three]).astype(jnp.int32)


def block_levels(stream_key, extent, pieces, low, top_value):
    level, own = 1.0, jax.random.fold_in(stream_key, 6)
    for dim, parts in pieces:
        draws = jnp.exp(jax.random.uniform(jax.random.fold_in(own, dim), (parts,), jnp.float32, low / len(pieces), top_value / len(pieces)))
        level = level * jnp.repeat(draws, extent[dim] // parts).reshape([-1 if axis == dim else 1 for axis in range(len(extent))])
    return level


def bell_draw(key, dims, scale, bound, cuts=(), kind=jnp.bfloat16):
    factor_of = block_levels(key, dims, cuts, -0.22, 0.18) if cuts else 1.0
    array = jax.random.normal(key, dims, jnp.float32) * scale * factor_of
    return jnp.minimum(jnp.maximum(array, -bound), bound).astype(kind)


def setup_inputs(seed: int = 0, part: int = 0) -> dict:
    splits = jax.random.split(jax.random.key(seed), 9)
    part_splits = jax.random.split(jax.random.fold_in(splits[8], part), 9)
    return {
        "tokens": draw_tokens(jax.random.fold_in(jax.random.fold_in(splits[8], part), 71), part),
        "tile_index": draw_tile_index(jax.random.fold_in(jax.random.fold_in(splits[8], part), 71), part),
        "dilation_offset": draw_dilation_offset(jax.random.fold_in(splits[8], 71), part),
        "norm_gain": draw_norm_gain(jax.random.fold_in(splits[8], 71), part),
        "w_query": bell_draw(splits[4], (D, D), D ** -0.5, 0.21875, ((1, 2),)),
        "w_key": bell_draw(splits[5], (D, D), D ** -0.5, 0.21875, ((1, 2),)),
        "w_value": bell_draw(splits[6], (D, D), D ** -0.5, 0.21875, ((1, 2),)),
        "w_out": bell_draw(splits[7], (D, D), D ** -0.5, 0.21875, ((0, 2),)),
    }


def position_table(tile_index):
    quarter = D // 4
    freq = jnp.exp(-jnp.log(10000.0) * jnp.arange(quarter, dtype=jnp.float32) / quarter)
    row_pos = (tile_index // GRID_W).astype(jnp.float32)[:, None] * freq[None, :]
    col_pos = (tile_index % GRID_W).astype(jnp.float32)[:, None] * freq[None, :]
    return jnp.concatenate([jnp.sin(row_pos), jnp.cos(row_pos), jnp.sin(col_pos), jnp.cos(col_pos)], axis=1)

def normalize(hidden, gain):
    mean = lax.optimization_barrier(jnp.mean(hidden, axis=1, keepdims=True))
    centred = hidden - mean
    spread = lax.optimization_barrier(jnp.mean(centred * centred, axis=1, keepdims=True))
    return (centred * lax.rsqrt(spread + 1e-05) * gain[None, :]).astype(jnp.bfloat16)

def attend(query_rows, key_rows, value_rows):
    score_scale = HEAD_DIM ** (-0.5)
    logit_scores = jnp.einsum('arl,ahl->arh', query_rows.astype(jnp.float32), key_rows.astype(jnp.float32)) * score_scale
    top = lax.optimization_barrier(jnp.max(logit_scores, axis=2, keepdims=True))
    weights = jnp.exp(logit_scores - top)
    total_length = lax.optimization_barrier(jnp.sum(weights, axis=2, keepdims=True))
    rounded_length = weights.astype(jnp.bfloat16).astype(jnp.float32)
    mixed = jnp.einsum('wfe,weu->wfu', rounded_length, value_rows.astype(jnp.float32)) / total_length
    return (mixed, top[..., 0] + jnp.log(total_length[..., 0]))

def branch(query_rows, key_rows, value_rows, rate, offset):

    def pick(x):
        taken = lax.dynamic_index_in_dim(x.reshape(SEQ // rate, rate, HEAD_DIM), offset, 1, keepdims=False)
        return taken.reshape(SEQ // rate // BLOCK, BLOCK, HEAD_DIM)
    mixed, lse = attend(pick(query_rows), pick(key_rows), pick(value_rows))
    chosen = jnp.arange(rate) == offset
    full = jnp.where(chosen[None, :, None], mixed.reshape(SEQ // rate, 1, HEAD_DIM), 0.0).reshape(SEQ, HEAD_DIM)
    lse_full = jnp.where(chosen[None, :], lse.reshape(SEQ // rate, 1), 0.0).reshape(SEQ)
    taken_mask = jnp.broadcast_to(chosen[None, :], (SEQ // rate, rate)).reshape(SEQ)
    return (full, lse_full, taken_mask)

def combine(out_one, lse_one, out_two, lse_two, mask_two, out_three, lse_three, mask_three):
    top = jnp.maximum(lse_one, jnp.where(mask_two, lse_two, lse_one))
    top = jnp.maximum(top, jnp.where(mask_three, lse_three, lse_one))
    weight_one = jnp.exp(lse_one - top)
    weight_two = jnp.where(mask_two, jnp.exp(lse_two - top), 0.0)
    weight_three = jnp.where(mask_three, jnp.exp(lse_three - top), 0.0)
    summed = weight_one[..., None] * out_one + weight_two[..., None] * out_two + weight_three[..., None] * out_three
    return summed / (weight_one + weight_two + weight_three)[..., None]

def reference(tokens, tile_index, dilation_offset, norm_gain, w_query, w_key, w_value, w_out):
    hidden = tokens.astype(jnp.float32) + position_table(tile_index)
    normed = normalize(hidden, norm_gain)
    query_rows = jnp.dot(normed, w_query, preferred_element_type=jnp.float32).astype(jnp.bfloat16)
    key_rows = jnp.dot(normed, w_key, preferred_element_type=jnp.float32).astype(jnp.bfloat16)
    value_rows = jnp.dot(normed, w_value, preferred_element_type=jnp.float32).astype(jnp.bfloat16)

    def one_head(args):
        head, offset_two, offset_three = args
        start = head * HEAD_DIM
        q_head = lax.dynamic_slice_in_dim(query_rows, start, HEAD_DIM, 1)
        k_head = lax.dynamic_slice_in_dim(key_rows, start, HEAD_DIM, 1)
        v_head = lax.dynamic_slice_in_dim(value_rows, start, HEAD_DIM, 1)
        out_one, lse_one, mask_one = branch(q_head, k_head, v_head, 1, 0)
        out_two, lse_two, mask_two = branch(q_head, k_head, v_head, R2, offset_two)
        out_three, lse_three, mask_three = branch(q_head, k_head, v_head, R3, offset_three)
        return combine(out_one, lse_one, out_two, lse_two, mask_two, out_three, lse_three, mask_three)
    heads = lax.map(one_head, (jnp.arange(HEADS, dtype=jnp.int32), dilation_offset[0], dilation_offset[1]))
    attn = heads.transpose(1, 0, 2).reshape(SEQ, D).astype(jnp.bfloat16)
    return hidden + jnp.dot(attn, w_out, preferred_element_type=jnp.float32)
```

```python
import functools
import math

import jax
import jax.numpy as jnp
import numpy as np
from jax import lax
from jax.experimental import pallas as pl
from jax.experimental.pallas import tpu as pltpu
from jax.sharding import PartitionSpec as P

D = 768
HEAD_DIM = 48
GRID_W = 256
LANES = 128
MESH = pl.DeviceIdType.MESH
F32 = jnp.float32
BF16 = jnp.bfloat16


def angle_tables(positions):
    quarter = D // 4
    freq = np.exp(
        -np.log(np.float32(10000.0)) * np.arange(quarter, dtype=np.float32) / np.float32(quarter)
    ).astype(np.float32)
    angle = np.asarray(positions, np.float32)[..., None] * freq
    return np.concatenate([np.sin(angle), np.cos(angle)], axis=-1).astype(np.float32)


def windows(heads):
    spans = []
    for head in range(heads):
        low = head * HEAD_DIM // LANES
        high = (head * HEAD_DIM + HEAD_DIM - 1) // LANES
        spans.append((low, high + 1))
    return spans


def lane_mask(head, low, high):
    lane = lax.broadcasted_iota(jnp.int32, (1, (high - low) * LANES), 1) + low * LANES
    return (lane >= head * HEAD_DIM) & (lane < (head + 1) * HEAD_DIM)


def attend_tile(query, load_keys, load_values, heads, width):
    rows = query.shape[0]
    tiles = width // LANES
    acc = [None] * tiles
    top = [None] * tiles
    tot = [None] * tiles
    factor = HEAD_DIM**-0.5 * math.log2(math.e)

    def put(store, tile, mask, part):
        part = jnp.broadcast_to(part, (rows, LANES))
        store[tile] = part if store[tile] is None else jnp.where(mask, part, store[tile])

    for head, (low, high) in enumerate(windows(heads)):
        mask = lane_mask(head, low, high)
        q = query[:, low * LANES : high * LANES]
        q = jnp.where(mask, q, jnp.zeros((), q.dtype))
        scores = lax.dot_general(
            q, load_keys(low, high), (((1,), (1,)), ((), ())), preferred_element_type=F32
        )
        best = jnp.max(scores, axis=1, keepdims=True)
        e = jnp.exp2((scores - best) * factor)
        total = jnp.sum(e, axis=1, keepdims=True)
        out = jnp.dot(e.astype(BF16), load_values(low, high), preferred_element_type=F32)
        for tile in range(low, high):
            at = slice((tile - low) * LANES, (tile - low + 1) * LANES)
            put(acc, tile, mask[:, at], out[:, at])
            put(top, tile, mask[:, at], best)
            put(tot, tile, mask[:, at], total)
    return tuple(jnp.concatenate(x, axis=1) for x in (acc, top, tot))


def kernel(
    n, rate_two, rate_three, heads,
    tokens_ref, index_ref, offset_ref, gain_ref, wq_ref, wk_ref, wv_ref, wo_ref, row_ref, col_ref,
    out_ref,
    hidden, query, query_two, query_three, kv, kv_in, kv_two, kv_three,
    acc_own, top_own, tot_own, acc_far, top_far, tot_far,
    acc_two, top_two, tot_two, acc_three, top_three, tot_three,
    attn, attn_in, wo_send, wo_in,
    sem_dense, sem_two, sem_three, sem_attn, sem_wo,
):
    rows = tokens_ref.shape[0]
    width = wq_ref.shape[1]
    me = lax.axis_index("seq")
    core = lax.axis_index("head")
    rows_two = rows // rate_two
    rows_three = rows // rate_three
    group = 2 * rate_two
    pairs = n // 2
    sub_pairs = group // 2
    side = lax.rem(me, 2)
    pair = me // 2
    base = (pair // sub_pairs) * sub_pairs
    inner = pair - base

    barrier = pltpu.get_barrier_semaphore()
    for step in range(1, n):
        pl.semaphore_signal(
            barrier, inc=1, device_id={"seq": lax.rem(me + step, n)}, device_id_type=MESH
        )
    pl.semaphore_signal(barrier, inc=1, device_id={"head": 1 - core}, device_id_type=MESH)

    def remote(src, dst, sems, slot, device):
        return pltpu.make_async_remote_copy(
            src_ref=src, dst_ref=dst, send_sem=sems.at[0, slot], recv_sem=sems.at[1, slot],
            device_id=device, device_id_type=MESH,
        )

    lane = lax.broadcasted_iota(jnp.int32, (1, rows), 1)
    line = lax.broadcasted_iota(jnp.int32, (rows, 1), 0)
    odd = jnp.sum(
        jnp.where(line == lane, (index_ref[...] & 1).astype(F32), 0.0), axis=1, keepdims=True
    )
    per = GRID_W // 2
    row_table = row_ref[me]
    half = D // 2
    for block in range(rows // per):
        at = slice(block * per, (block + 1) * per)
        hidden[at, :half] = tokens_ref[at, :half].astype(F32) + row_table[block : block + 1, :]
        hidden[at, half:] = tokens_ref[at, half:].astype(F32) + jnp.where(
            odd[at] > 0.5, col_ref[1], col_ref[0]
        )
    h = hidden[...]
    mean = jnp.mean(h, axis=1, keepdims=True)
    centred = h - mean
    spread = jnp.mean(centred * centred, axis=1, keepdims=True)
    normed = (centred * lax.rsqrt(spread + 1e-05) * gain_ref[...]).astype(BF16)

    def source_of(i):
        c = i // rows_two
        rest = i - c * rows_two
        b = rest // rows_three
        a = rest - b * rows_three
        return a * rate_three + b * rate_two + c

    order = jnp.where(source_of(line) == lane, 1.0, 0.0).astype(BF16)
    normed = jnp.dot(order, normed, preferred_element_type=F32).astype(BF16)
    kv[:, :width] = jnp.dot(normed, wk_ref[...], preferred_element_type=F32).astype(BF16)
    kv[:, width:] = jnp.dot(normed, wv_ref[...], preferred_element_type=F32).astype(BF16)

    head_of = lax.broadcasted_iota(jnp.int32, (1, width), 1) // HEAD_DIM
    off_two = jnp.zeros((1, width), jnp.int32)
    off_three = jnp.zeros((1, width), jnp.int32)
    for head in range(heads):
        off_two = jnp.where(head_of == head, offset_ref[0, head], off_two)
        off_three = jnp.where(head_of == head, offset_ref[1, head], off_three)

    def class_mask(offset, index, rate):
        residue = index if rate == rate_two else (
            index // (rate_three // rate_two) + rate_two * (index % (rate_three // rate_two))
        )
        return offset == residue

    def select(ref, at, offset, rate):
        count = rows // rate
        out = ref[0:count, at]
        for index in range(1, rate):
            out = jnp.where(
                class_mask(offset, index, rate), ref[index * count : (index + 1) * count, at], out
            )
        return out

    keys_at, values_at = slice(0, width), slice(width, 2 * width)

    def select_kv(ref, buffer, slot, offset, rate):
        buffer[slot, :, keys_at] = select(ref, keys_at, offset, rate)
        buffer[slot, :, values_at] = select(ref, values_at, offset, rate)

    wo_send[...] = wo_ref[:, pl.ds(pl.multiple_of((1 - core) * width, width), width)]
    select_kv(kv, kv_two, 0, off_two, rate_two)
    select_kv(kv, kv_three, 0, off_three, rate_three)

    pl.semaphore_wait(barrier, n)
    copies = []

    def begin(copy):
        copy.start()
        copies.append(copy)
        return copy

    dense = begin(remote(kv, kv_in, sem_dense, 0, {"seq": me + 1 - 2 * side}))
    two, three = [], []
    for step in range(1, sub_pairs):
        for flip in range(2):
            slot = 2 * step + flip
            target = 2 * (base + lax.rem(inner + step, sub_pairs)) + lax.rem(side + flip, 2)
            two.append(
                begin(remote(kv_two.at[0], kv_two.at[slot], sem_two, slot, {"seq": target}))
            )
    for step in range(1, pairs):
        for flip in range(2):
            slot = 2 * step + flip
            target = 2 * lax.rem(pair + step, pairs) + lax.rem(side + flip, 2)
            three.append(
                begin(remote(kv_three.at[0], kv_three.at[slot], sem_three, slot, {"seq": target}))
            )
    wo_copy = begin(remote(wo_send, wo_in, sem_wo, 0, {"head": 1 - core}))

    query[...] = jnp.dot(normed, wq_ref[...], preferred_element_type=F32).astype(BF16)
    query_two[...] = select(query, keys_at, off_two, rate_two)
    query_three[...] = select(query, keys_at, off_three, rate_three)

    def flat_loader(ref, start):
        return lambda low, high: ref[:, start + low * LANES : start + high * LANES]

    def slot_loader(ref, start):
        def load(low, high):
            x = ref[:, :, start + low * LANES : start + high * LANES]
            slots, count, span = x.shape
            if count % 16:
                x = x.astype(F32)
            return x.reshape(slots * count, span).astype(BF16)

        return load

    def run(q_ref, keys, values, acc, top, tot):
        total = q_ref.shape[0]
        tile = min(128, total)

        def step(i, carry):
            at = pl.ds(pl.multiple_of(i * tile, tile), tile)
            a, m, t = attend_tile(q_ref[at, :], keys, values, heads, width)
            acc[at, :] = a
            top[at, :] = m
            tot[at, :] = t
            return carry

        if total == tile:
            a, m, t = attend_tile(q_ref[...], keys, values, heads, width)
            acc[...] = a
            top[...] = m
            tot[...] = t
        else:
            lax.fori_loop(0, total // tile, step, 0)

    run(query, flat_loader(kv, 0), flat_loader(kv, width), acc_own, top_own, tot_own)
    dense.wait_recv()
    select_kv(kv_in, kv_two, 1, off_two, rate_two)
    select_kv(kv_in, kv_three, 1, off_three, rate_three)
    run(query, flat_loader(kv_in, 0), flat_loader(kv_in, width), acc_far, top_far, tot_far)
    for copy in two:
        copy.wait_recv()
    run(query_two, slot_loader(kv_two, 0), slot_loader(kv_two, width), acc_two, top_two, tot_two)
    for copy in three:
        copy.wait_recv()
    run(
        query_three, slot_loader(kv_three, 0), slot_loader(kv_three, width),
        acc_three, top_three, tot_three,
    )

    factor = HEAD_DIM**-0.5 * math.log2(math.e)
    ratio = rate_three // rate_two
    for block in range(rate_three):
        at = slice(block * rows_three, (block + 1) * rows_three)
        inner_at = slice((block % ratio) * rows_three, (block % ratio + 1) * rows_three)
        takes_two = class_mask(off_two, block // ratio, rate_two)
        takes_three = class_mask(off_three, block, rate_three)
        m_own, m_far = top_own[at, :], top_far[at, :]
        best = jnp.maximum(m_own, m_far)
        m_two = jnp.where(takes_two, top_two[inner_at, :], m_own)
        m_three = jnp.where(takes_three, top_three[...], m_own)
        best = jnp.maximum(jnp.maximum(best, m_two), m_three)
        u_own = jnp.exp2((m_own - best) * factor)
        u_far = jnp.exp2((m_far - best) * factor)
        u_two = jnp.where(takes_two, jnp.exp2((m_two - best) * factor), 0.0)
        u_three = jnp.where(takes_three, jnp.exp2((m_three - best) * factor), 0.0)
        summed = (
            u_own * acc_own[at, :] + u_far * acc_far[at, :]
            + u_two * acc_two[inner_at, :] + u_three * acc_three[...]
        )
        total = (
            u_own * tot_own[at, :] + u_far * tot_far[at, :]
            + u_two * tot_two[inner_at, :] + u_three * tot_three[...]
        )
        hidden_rows = summed / total
        acc_own[at, :] = hidden_rows
    back = jnp.where(source_of(lane) == line, 1.0, 0.0).astype(BF16)
    attn[...] = jnp.dot(back, acc_own[...].astype(BF16), preferred_element_type=F32).astype(BF16)
    attn_copy = begin(remote(attn, attn_in, sem_attn, 0, {"head": 1 - core}))
    mine = pl.ds(pl.multiple_of(core * width, width), width)
    out_ref[...] = hidden[:, mine] + jnp.dot(
        attn[...], wo_ref[:, mine], preferred_element_type=F32
    )
    wo_copy.wait_recv()
    attn_copy.wait_recv()
    out_ref[...] += jnp.dot(attn_in[...], wo_in[...], preferred_element_type=F32)
    for copy in copies:
        copy.wait_send()


def body(n, tokens, tile_index, dilation_offset, norm_gain, w_query, w_key, w_value, w_out):
    rows = tokens.shape[0]
    width = w_query.shape[1]
    heads = width // HEAD_DIM
    rate_two = min(16, n // 4)
    rate_three = n // 2
    per = GRID_W // 2
    grid_rows = rows // per
    row_table = jnp.asarray(
        angle_tables(np.arange(n * grid_rows).reshape(n, grid_rows)), F32
    )
    col_table = jnp.asarray(angle_tables(np.arange(GRID_W).reshape(per, 2).T), F32)
    rows_two, rows_three = rows // rate_two, rows // rate_three
    group = 2 * rate_two
    vmem = pl.BlockSpec(memory_space=pltpu.VMEM)

    def trio(count):
        return [pltpu.VMEM((count, width), F32)] * 3

    return pl.pallas_call(
        functools.partial(kernel, n, rate_two, rate_three, heads),
        out_shape=jax.ShapeDtypeStruct((rows, width), F32),
        in_specs=[
            vmem, vmem, pl.BlockSpec(memory_space=pltpu.SMEM), vmem, vmem, vmem, vmem, vmem,
            vmem, vmem,
        ],
        out_specs=vmem,
        scratch_shapes=[
            pltpu.VMEM((rows, D), F32),
            pltpu.VMEM((rows, width), BF16),
            pltpu.VMEM((rows_two, width), BF16),
            pltpu.VMEM((rows_three, width), BF16),
            pltpu.VMEM((rows, 2 * width), BF16),
            pltpu.VMEM((rows, 2 * width), BF16),
            pltpu.VMEM((group, rows_two, 2 * width), BF16),
            pltpu.VMEM((n, rows_three, 2 * width), BF16),
            *trio(rows), *trio(rows), *trio(rows_two), *trio(rows_three),
            pltpu.VMEM((rows, width), BF16),
            pltpu.VMEM((rows, width), BF16),
            pltpu.VMEM((width, width), BF16),
            pltpu.VMEM((width, width), BF16),
            pltpu.SemaphoreType.DMA((2, 1)),
            pltpu.SemaphoreType.DMA((2, group)),
            pltpu.SemaphoreType.DMA((2, n)),
            pltpu.SemaphoreType.DMA((2, 1)),
            pltpu.SemaphoreType.DMA((2, 1)),
        ],
        compiler_params=pltpu.CompilerParams(
            collective_id=0, has_side_effects=True, vmem_limit_bytes=48 * 1024 * 1024
        ),
    )(
        tokens, tile_index.reshape(1, rows), dilation_offset, norm_gain.reshape(1, D),
        w_query, w_key, w_value, w_out, row_table, col_table,
    )


def solution(mesh):
    placed = (
        P(("slide", "seq"), None),
        P(("slide", "seq")),
        P(None, "head"),
        P(),
        P(None, "head"),
        P(None, "head"),
        P(None, "head"),
        P("head", None),
    )
    return jax.shard_map(
        functools.partial(body, mesh.shape["seq"]), mesh=mesh, in_specs=placed,
        out_specs=P(("slide", "seq"), "head"), check_vma=False,
    )
```

```python
import functools
import math

import jax
import jax.numpy as jnp
import numpy as np
from jax import lax
from jax.experimental import pallas as pl
from jax.experimental.pallas import tpu as pltpu
from jax.sharding import PartitionSpec as P

D = 768
HEAD_DIM = 48
GRID_W = 256
LANES = 128
MESH = pl.DeviceIdType.MESH
F32 = jnp.float32
BF16 = jnp.bfloat16


def angle_tables(positions):
    quarter = D // 4
    freq = np.exp(
        -np.log(np.float32(10000.0)) * np.arange(quarter, dtype=np.float32) / np.float32(quarter)
    ).astype(np.float32)
    angle = np.asarray(positions, np.float32)[..., None] * freq
    return np.concatenate([np.sin(angle), np.cos(angle)], axis=-1).astype(np.float32)


def windows(heads):
    spans = []
    for head in range(heads):
        low = head * HEAD_DIM // LANES
        high = (head * HEAD_DIM + HEAD_DIM - 1) // LANES
        spans.append((low, high + 1))
    return spans


def lane_mask(head, low, high):
    lane = lax.broadcasted_iota(jnp.int32, (1, (high - low) * LANES), 1) + low * LANES
    return (lane >= head * HEAD_DIM) & (lane < (head + 1) * HEAD_DIM)


def attend_tile(query, load_keys, load_values, heads, width, packed):
    rows = query.shape[0]
    tiles = width // LANES
    acc = [None] * tiles
    top = [None] * tiles
    tot = [None] * tiles
    stat = jnp.zeros((rows, LANES), F32)
    stat_lane = lax.broadcasted_iota(jnp.int32, (1, LANES), 1)
    factor = HEAD_DIM**-0.5 * math.log2(math.e)

    def put(store, tile, mask, part):
        part = jnp.broadcast_to(part, (rows, LANES))
        store[tile] = part if store[tile] is None else jnp.where(mask, part, store[tile])

    for head, (low, high) in enumerate(windows(heads)):
        mask = lane_mask(head, low, high)
        q = query[:, low * LANES : high * LANES]
        q = jnp.where(mask, q, jnp.zeros((), q.dtype))
        scores = lax.dot_general(
            q, load_keys(low, high), (((1,), (1,)), ((), ())), preferred_element_type=F32
        )
        best = jnp.max(scores, axis=1, keepdims=True)
        e = jnp.exp2((scores - best) * factor)
        total = jnp.sum(e, axis=1, keepdims=True)
        out = jnp.dot(e.astype(BF16), load_values(low, high), preferred_element_type=F32)
        for tile in range(low, high):
            at = slice((tile - low) * LANES, (tile - low + 1) * LANES)
            put(acc, tile, mask[:, at], out[:, at])
            put(top, tile, mask[:, at], best)
            put(tot, tile, mask[:, at], total)
        if packed:
            stat = jnp.where(stat_lane == head, best, stat)
            stat = jnp.where(stat_lane == LANES // 2 + head, total, stat)
    return tuple(jnp.concatenate(x, axis=1) for x in (acc, top, tot)) + (stat,)


def kernel(
    n, rate_two, rate_three, heads,
    tokens_hbm, index_ref, offset_ref, gain_ref, wq_hbm, wk_hbm, wv_hbm, wo_hbm, row_hbm, col_hbm,
    out_ref,
    tokens_ref, wq_ref, wk_ref, wv_ref, wo_ref, row_ref, col_ref,
    hidden, nrm, nrm_in, query, query_far, query_two, query_three, kv, kv_in, kv_two, kv_three,
    acc_own, top_own, tot_own, acc_far, top_far, tot_far,
    acc_two, top_two, tot_two, acc_three, top_three, tot_three,
    stat_two, stat_three, ret_two, ret_three,
    back_two, back_three, back_stat_two, back_stat_three,
    attn, attn_in, wo_send, wo_in,
    sem_load, sem_dense, sem_two, sem_three, sem_pair,
):
    rows = tokens_ref.shape[0]
    width = wq_ref.shape[1]
    me = lax.axis_index("seq")
    core = lax.axis_index("head")
    rows_two = rows // rate_two
    rows_three = rows // rate_three
    pairs = n // 2
    sub_pairs = rate_two
    side = lax.rem(me, 2)
    pair = me // 2
    base = (pair // sub_pairs) * sub_pairs
    inner = pair - base
    partner = {"seq": me + 1 - 2 * side}
    sibling = {"head": 1 - core}

    loads = []
    for slot, (src, dst) in enumerate((
        (tokens_hbm, tokens_ref), (row_hbm.at[me], row_ref), (col_hbm, col_ref),
        (wk_hbm, wk_ref), (wv_hbm, wv_ref), (wq_hbm, wq_ref), (wo_hbm, wo_ref),
    )):
        load = pltpu.make_async_copy(src, dst, sem_load.at[slot])
        load.start()
        loads.append(load)

    barrier = pltpu.get_barrier_semaphore()
    for step in range(1, pairs):
        pl.semaphore_signal(
            barrier, inc=1, device_id={"seq": 2 * lax.rem(pair + step, pairs) + side},
            device_id_type=MESH,
        )
    pl.semaphore_signal(barrier, inc=1, device_id=partner, device_id_type=MESH)
    pl.semaphore_signal(barrier, inc=1, device_id=sibling, device_id_type=MESH)

    def remote(src, dst, sems, slot, device):
        return pltpu.make_async_remote_copy(
            src_ref=src, dst_ref=dst, send_sem=sems.at[0, slot], recv_sem=sems.at[1, slot],
            device_id=device, device_id_type=MESH,
        )

    copies = []

    def begin(copy):
        copy.start()
        copies.append(copy)
        return copy

    lane = lax.broadcasted_iota(jnp.int32, (1, rows), 1)
    line = lax.broadcasted_iota(jnp.int32, (rows, 1), 0)

    def source_of(i):
        c = i // rows_two
        rest = i - c * rows_two
        b = rest // rows_three
        a = rest - b * rows_three
        return a * rate_three + b * rate_two + c

    order = jnp.where(source_of(line) == lane, 1.0, 0.0).astype(BF16)

    odd = jnp.sum(
        jnp.where(line == lane, (index_ref[...].reshape(1, rows) & 1).astype(F32), 0.0),
        axis=1, keepdims=True,
    )
    per = GRID_W // 2
    half = D // 2
    for load in loads[:3]:
        load.wait()
    for block in range(rows // per):
        at = slice(block * per, (block + 1) * per)
        hidden[at, :half] = tokens_ref[at, :half].astype(F32) + row_ref[block : block + 1, :]
        hidden[at, half:] = tokens_ref[at, half:].astype(F32) + jnp.where(
            odd[at] > 0.5, col_ref[1], col_ref[0]
        )
    h = hidden[...]
    mean = jnp.mean(h, axis=1, keepdims=True)
    centred = h - mean
    spread = jnp.mean(centred * centred, axis=1, keepdims=True)
    normed = (
        centred * lax.rsqrt(spread + 1e-05) * gain_ref[...].reshape(1, D)
    ).astype(BF16)
    nrm[...] = jnp.dot(order, normed, preferred_element_type=F32).astype(BF16)

    part = pl.ds(pl.multiple_of(core * (rows // 2), rows // 2), rows // 2)
    pl.semaphore_wait(barrier, pairs + 1)
    dense = begin(remote(nrm.at[part], nrm_in.at[part], sem_dense, 0, partner))
    share = remote(nrm_in.at[part], nrm_in.at[part], sem_dense, 1, sibling)

    def project(source, w_ref):
        return jnp.dot(source[...], w_ref[...], preferred_element_type=F32).astype(BF16)

    for load in loads[3:]:
        load.wait()
    kv[:, :width] = project(nrm, wk_ref)
    kv[:, width:] = project(nrm, wv_ref)

    head_of = lax.broadcasted_iota(jnp.int32, (1, width), 1) // HEAD_DIM
    off_two = jnp.zeros((1, width), jnp.int32)
    off_three = jnp.zeros((1, width), jnp.int32)
    for head in range(heads):
        off_two = jnp.where(head_of == head, offset_ref[0, head], off_two)
        off_three = jnp.where(head_of == head, offset_ref[1, head], off_three)

    def class_mask(offset, index, rate):
        residue = index if rate == rate_two else (
            index // (rate_three // rate_two) + rate_two * (index % (rate_three // rate_two))
        )
        return offset == residue

    def select(ref, at, offset, rate):
        count = rows // rate
        out = ref[0:count, at]
        for index in range(1, rate):
            out = jnp.where(
                class_mask(offset, index, rate), ref[index * count : (index + 1) * count, at], out
            )
        return out

    keys_at, values_at = slice(0, width), slice(width, 2 * width)

    def select_kv(ref, buffer, slot, offset, rate):
        buffer[slot, :, keys_at] = select(ref, keys_at, offset, rate)
        buffer[slot, :, values_at] = select(ref, values_at, offset, rate)

    select_kv(kv, kv_two, 0, off_two, rate_two)
    two, three = [], []
    for step in range(1, sub_pairs):
        target = 2 * (base + lax.rem(inner + step, sub_pairs)) + side
        two.append(begin(remote(kv_two.at[0], kv_two.at[step], sem_two, step, {"seq": target})))
    select_kv(kv, kv_three, 0, off_three, rate_three)
    for step in range(1, pairs):
        target = 2 * lax.rem(pair + step, pairs) + side
        three.append(
            begin(remote(kv_three.at[0], kv_three.at[step], sem_three, step, {"seq": target}))
        )
    wo_send[...] = wo_ref[:, pl.ds(pl.multiple_of((1 - core) * width, width), width)]
    wo_copy = begin(remote(wo_send, wo_in, sem_pair, 0, sibling))

    query[...] = project(nrm, wq_ref)
    query_two[0] = select(query, keys_at, off_two, rate_two)
    query_three[0] = select(query, keys_at, off_three, rate_three)

    def flat_loader(ref, start):
        return lambda low, high: ref[:, start + low * LANES : start + high * LANES]

    def slot_loader(ref, start):
        def load(low, high):
            x = ref[:, :, start + low * LANES : start + high * LANES]
            slots, count, span = x.shape
            if count % 16:
                x = x.astype(F32)
            return x.reshape(slots * count, span).astype(BF16)

        return load

    def run(read, total, tile, keys, values, store, packed=False):
        def step(i, carry):
            store(i, *attend_tile(read(i), keys, values, heads, width, packed))
            return carry

        lax.fori_loop(0, total // tile, step, 0)

    def run_dense(keys_ref, acc, top, tot):
        tile = min(128, rows)

        def at(i):
            return pl.ds(pl.multiple_of(i * tile, tile), tile)

        def store(i, a, m, t, stat):
            acc[at(i), :] = a
            top[at(i), :] = m
            tot[at(i), :] = t

        run(
            lambda i: query[at(i), :], rows, tile, flat_loader(keys_ref, 0),
            flat_loader(keys_ref, width), store,
        )

    def run_slots(q_ref, keys_ref, acc, top, tot, stat):
        count = q_ref.shape[1]
        tile = min(128, count)
        each = count // tile

        def at(i):
            return pl.ds(pl.multiple_of(lax.rem(i, each) * tile, tile), tile)

        def store(i, a, m, t, s):
            acc[i // each, at(i), :] = a
            top[i // each, at(i), :] = m
            tot[i // each, at(i), :] = t
            stat[i // each, at(i), :] = s

        run(
            lambda i: q_ref[i // each, at(i), :], 2 * count, tile, slot_loader(keys_ref, 0),
            slot_loader(keys_ref, width), store, True,
        )

    run_dense(kv, acc_own, top_own, tot_own)
    dense.wait_recv()
    begin(share).wait_recv()
    query_far[...] = project(nrm_in, wq_ref)
    query_two[1] = select(query_far, keys_at, off_two, rate_two)
    query_three[1] = select(query_far, keys_at, off_three, rate_three)
    for copy in two:
        copy.wait_recv()
    run_slots(query_two, kv_two, acc_two, top_two, tot_two, stat_two)
    ret_two[...] = acc_two[1].astype(BF16)
    back = [
        begin(remote(ret_two, back_two, sem_pair, 2, partner)),
        begin(remote(stat_two.at[1], back_stat_two, sem_pair, 3, partner)),
    ]
    kv_in[:, :width] = project(nrm_in, wk_ref)
    kv_in[:, width:] = project(nrm_in, wv_ref)
    for copy in three:
        copy.wait_recv()
    run_slots(query_three, kv_three, acc_three, top_three, tot_three, stat_three)
    ret_three[...] = acc_three[1].astype(BF16)
    back.append(begin(remote(ret_three, back_three, sem_pair, 4, partner)))
    back.append(begin(remote(stat_three.at[1], back_stat_three, sem_pair, 5, partner)))
    run_dense(kv_in, acc_far, top_far, tot_far)
    for copy in back:
        copy.wait_recv()

    def spread(stat, start):
        out = jnp.zeros((stat.shape[0], width), F32)
        for head in range(heads):
            out = jnp.where(head_of == head, stat[:, start + head : start + head + 1], out)
        return out

    factor = HEAD_DIM**-0.5 * math.log2(math.e)

    def merge(terms):
        best = functools.reduce(jnp.maximum, [m for _, m, _ in terms])
        acc = tot = 0.0
        for a, m, t in terms:
            u = jnp.exp2((m - best) * factor)
            acc = acc + u * a
            tot = tot + u * t
        return acc, best, tot

    def join(acc, top, tot, back_acc, back_stat):
        far = back_stat[...]
        a, m, t = merge([
            (acc[0], top[0], tot[0]),
            (back_acc[...].astype(F32), spread(far, 0), spread(far, LANES // 2)),
        ])
        acc[0] = a
        top[0] = m
        tot[0] = t

    join(acc_two, top_two, tot_two, back_two, back_stat_two)
    join(acc_three, top_three, tot_three, back_three, back_stat_three)
    ratio = rate_three // rate_two
    for block in range(rate_three):
        at = slice(block * rows_three, (block + 1) * rows_three)
        inner_at = slice((block % ratio) * rows_three, (block % ratio + 1) * rows_three)
        takes_two = class_mask(off_two, block // ratio, rate_two)
        takes_three = class_mask(off_three, block, rate_three)
        m_own, m_far = top_own[at, :], top_far[at, :]
        m_two, m_three = top_two[0, inner_at, :], top_three[0]
        acc, _, tot = merge([
            (acc_own[at, :], m_own, tot_own[at, :]),
            (acc_far[at, :], m_far, tot_far[at, :]),
            (
                jnp.where(takes_two, acc_two[0, inner_at, :], 0.0),
                jnp.where(takes_two, m_two, m_own),
                jnp.where(takes_two, tot_two[0, inner_at, :], 0.0),
            ),
            (
                jnp.where(takes_three, acc_three[0], 0.0),
                jnp.where(takes_three, m_three, m_own),
                jnp.where(takes_three, tot_three[0], 0.0),
            ),
        ])
        acc_own[at, :] = acc / tot
    undo = jnp.where(source_of(lane) == line, 1.0, 0.0).astype(BF16)
    attn[...] = jnp.dot(undo, acc_own[...].astype(BF16), preferred_element_type=F32).astype(BF16)
    attn_copy = begin(remote(attn, attn_in, sem_pair, 1, sibling))
    mine = pl.ds(pl.multiple_of(core * width, width), width)
    out_ref[...] = hidden[:, mine] + jnp.dot(
        attn[...], wo_ref[:, mine], preferred_element_type=F32
    )
    wo_copy.wait_recv()
    attn_copy.wait_recv()
    out_ref[...] += jnp.dot(attn_in[...], wo_in[...], preferred_element_type=F32)
    for copy in copies:
        copy.wait_send()


def body(n, tokens, tile_index, dilation_offset, norm_gain, w_query, w_key, w_value, w_out):
    rows = tokens.shape[0]
    width = w_query.shape[1]
    heads = width // HEAD_DIM
    rate_two = min(16, n // 4)
    rate_three = n // 2
    per = GRID_W // 2
    grid_rows = rows // per
    row_table = jnp.asarray(
        angle_tables(np.arange(n * grid_rows).reshape(n, grid_rows)), F32
    )
    col_table = jnp.asarray(angle_tables(np.arange(GRID_W).reshape(per, 2).T), F32)
    rows_two, rows_three = rows // rate_two, rows // rate_three
    vmem = pl.BlockSpec(memory_space=pltpu.VMEM)
    hbm = pl.BlockSpec(memory_space=pltpu.HBM)

    def trio(*shape):
        return [pltpu.VMEM((*shape, width), F32)] * 3

    def narrow(*shape):
        return pltpu.VMEM(shape, BF16)

    return pl.pallas_call(
        functools.partial(kernel, n, rate_two, rate_three, heads),
        out_shape=jax.ShapeDtypeStruct((rows, width), F32),
        in_specs=[
            hbm, vmem, pl.BlockSpec(memory_space=pltpu.SMEM), vmem, hbm, hbm, hbm, hbm, hbm, hbm
        ],
        out_specs=vmem,
        scratch_shapes=[
            narrow(rows, D), narrow(D, width), narrow(D, width), narrow(D, width),
            narrow(width, D), pltpu.VMEM((grid_rows, D // 2), F32),
            pltpu.VMEM((2, per, D // 2), F32),
            pltpu.VMEM((rows, D), F32), narrow(rows, D), narrow(rows, D),
            narrow(rows, width), narrow(rows, width),
            narrow(2, rows_two, width), narrow(2, rows_three, width),
            narrow(rows, 2 * width), narrow(rows, 2 * width),
            narrow(rate_two, rows_two, 2 * width), narrow(n // 2, rows_three, 2 * width),
            *trio(rows), *trio(rows), *trio(2, rows_two), *trio(2, rows_three),
            pltpu.VMEM((2, rows_two, LANES), F32), pltpu.VMEM((2, rows_three, LANES), F32),
            narrow(rows_two, width), narrow(rows_three, width),
            narrow(rows_two, width), narrow(rows_three, width),
            pltpu.VMEM((rows_two, LANES), F32), pltpu.VMEM((rows_three, LANES), F32),
            narrow(rows, width), narrow(rows, width),
            narrow(width, width), narrow(width, width),
            pltpu.SemaphoreType.DMA((7,)),
            pltpu.SemaphoreType.DMA((2, 2)),
            pltpu.SemaphoreType.DMA((2, rate_two)),
            pltpu.SemaphoreType.DMA((2, n // 2)),
            pltpu.SemaphoreType.DMA((2, 6)),
        ],
        compiler_params=pltpu.CompilerParams(
            collective_id=0, has_side_effects=True, vmem_limit_bytes=48 * 1024 * 1024
        ),
    )(
        tokens, tile_index, dilation_offset, norm_gain,
        w_query, w_key, w_value, w_out, row_table, col_table,
    )


def solution(mesh):
    placed = (
        P(("slide", "seq"), None),
        P(("slide", "seq")),
        P(None, "head"),
        P(),
        P(None, "head"),
        P(None, "head"),
        P(None, "head"),
        P("head", None),
    )
    return jax.shard_map(
        functools.partial(body, mesh.shape["seq"]), mesh=mesh, in_specs=placed,
        out_specs=P(("slide", "seq"), "head"), check_vma=False,
    )
```
